256 devices in a mesh: group: 16 (over x, y_lo, core), seq: 16 (over z, y_hi).
Axes of the slice: x: 4, y: 4 (y_hi: 2, y_lo: 2; y = y_hi * 2 + y_lo), z: 8, core: 2. Of those that a mesh axis runs over, the one named last changes fastest.
Arguments:
- residual: bfloat16 [16, 1024, 4608], P('group', 'seq'), may hold values from -6 to 6
- cand_qkv: bfloat16 [16, 1024, 16, 512], P('group', 'seq'), may hold values from -80 to 80
- prompt_kv: bfloat16 [16, 2048, 16, 256], P(None, 'group', 'seq'), may hold values from -4 to 4
- prompt_len: int32 [16], replicated, may hold values from 1 to 2048, 17408 in all
- cand_prompt: int32 [16], replicated, may hold values from 0 to 15, as said below
- out_weight: bfloat16 [4096, 4608], P('seq'), may hold values from -0.09375 to 0.09375
- post_gain: float32 [4608], replicated, may hold values from 0.5 to 1.5
Outputs:
- layer_out: bfloat16 [16, 1024, 4608], P('group', 'seq')
The draws below stay inside these ranges and needn't reach their ends.
Inputs may be any that keep to these rules, and one draw needn't show every extreme that they name: `cand_prompt`: each of the 16 prompts is named by exactly one candidate.
All inputs are finite; a program needn't handle non-finite values.
Results may differ from the reference program's by a relative error of at most 0.017.
Values may be sent and summed in bfloat16 or wider, within the bound.
No kernel may reach another device: no remote copies, remote signals or barrier semaphores. Data moves between devices by JAX's collectives and lax.ppermute only.
A program may use at most 128 MiB of HBM per device.

```python
import math
import jax
import jax.numpy as jnp
import numpy as np
from jax import lax

D = 4608
H = 32
HD = 128
KVH = 16
CLEN = 1024
PLEN = 2048
PROMPTS = 16
CANDS = 16
N_SEQ = 16


def draw_cand_prompt(key, part):
    key = jax.random.fold_in(key, 5)
    order = jax.random.permutation(key, CANDS)
    return (order % PROMPTS).astype(jnp.int32)


def draw_cand_qkv(key, part):
    key = jax.random.fold_in(key, 7)
    base_key = jax.random.fold_in(key, 0)
    q_per_kv = H // KVH
    shape = (CANDS, CLEN, KVH, (q_per_kv + 2) * HD)
    base = jnp.clip(jax.random.normal(base_key, shape, jnp.float32), -4.0, 4.0)
    return base.astype(jnp.bfloat16)


def levels(key, extent, shards, smallest, top_value):
    def one(axis_at, shards_of):
        draws = jax.random.uniform(jax.random.fold_in(jax.random.fold_in(key, 6), axis_at), (shards_of,), jnp.float32, smallest / len(shards), top_value / len(shards))
        return jnp.repeat(jnp.exp(draws), extent[axis_at] // shards_of).reshape((-1,) + (1,) * (len(extent) - axis_at - 1))

    factor_of = one(*shards[0])
    for cut in shards[1:]:
        factor_of = factor_of * one(*cut)
    return factor_of


def profile(number_of, total, most, skew):
    portions = [(1 << 20) // math.isqrt(rank ** skew) + 1 for rank in range(2, number_of + 1)]
    spare, given = total - most - (number_of - 1), [1] * (number_of - 1)
    while spare > 0:
        free = [i for i in range(number_of - 1) if given[i] < most]
        pool, budget = sum([portions[i] for i in free]), spare
        for i in free:
            addition = min(most - given[i], max(1, budget * portions[i] // pool), spare)
            given[i] = given[i] + addition
            spare = spare - addition
    return np.array([most] + given)


def ragged_sizes(stream_key, number_of, total, most, slope):
    if number_of == 2:
        one = jax.random.randint(stream_key, (), max(1, total - most), min(most, total - 1) + 1)
        return jnp.stack([one, total - one])
    lengths = jnp.asarray(profile(number_of, total, most, slope), jnp.int32)
    twos = (number_of - 1) // 2
    donor, taker = lengths[1:1 + 2 * twos:2], lengths[2:2 + 2 * twos:2]
    slack = jnp.minimum(donor - 1, most - taker)
    passed = jax.random.randint(jax.random.fold_in(stream_key, 1), (twos,), 0, 1 << 20) % (slack + 1)
    lengths = lengths.at[1:1 + 2 * twos:2].set(donor - passed).at[2:2 + 2 * twos:2].set(taker + passed)
    return lengths[jax.random.permutation(jax.random.fold_in(stream_key, 2), number_of)]


def normal_values(rng, shape, width, bound, cuts=(), kind=jnp.bfloat16):
    values = jax.random.normal(rng, shape, jnp.float32) * width
    if len(cuts) > 0:
        values = levels(rng, shape, cuts, -0.22, 0.18) * values
    return jnp.clip(values, min=-bound, max=bound).astype(kind)


def setup_inputs(seed: int = 0) -> dict:
    keys = jax.random.split(jax.random.key(seed), 8)
    residual = normal_values(keys[0], (CANDS, CLEN, D), 1.0, 6.0, ((0, 16), (1, 16)))
    cand_qkv = draw_cand_qkv(jax.random.fold_in(keys[7], 71), 0)
    prompt_kv = normal_values(keys[2], (PROMPTS, PLEN, KVH, 2 * HD), 1.0, 4.0, ((1, 16), (2, 16)))
    prompt_len = ragged_sizes(keys[3], PROMPTS, PLEN + (PROMPTS - 1) * PLEN // 2, PLEN, 1).astype(jnp.int32)
    cand_prompt = draw_cand_prompt(jax.random.fold_in(keys[7], 71), 0)
    out_weight = normal_values(keys[5], (H * HD, D), (H * HD) ** -0.5, 0.09375, ((0, 16),))
    post_gain = jnp.clip(1.0 + 0.1 * jax.random.normal(keys[6], (D,), jnp.float32), 0.5, 1.5)
    return dict(residual=residual, cand_qkv=cand_qkv, prompt_kv=prompt_kv, prompt_len=prompt_len, cand_prompt=cand_prompt, out_weight=out_weight, post_gain=post_gain)


QUERY_SCALE = 144.0 ** (-0.5)
NORM_EPS = 1e-06
NEG_FILL = -1e+30

def score_one(residual, qkv_rows, prompt_id, prompt_kv, prompt_len, out_weight, post_gain):
    q_per_kv = H // KVH
    qkv_float = qkv_rows.astype(jnp.float32)
    queries = qkv_float[:, :, :q_per_kv * HD].reshape(CLEN, KVH, q_per_kv, HD)
    key_rows = qkv_float[:, :, q_per_kv * HD:(q_per_kv + 1) * HD]
    value_rows = qkv_float[:, :, (q_per_kv + 1) * HD:]
    prompt_rows = prompt_kv[prompt_id].astype(jnp.float32)
    prompt_keys = prompt_rows[:, :, :HD]
    prompt_values = prompt_rows[:, :, HD:]
    limit = prompt_len[prompt_id]
    prefix = jnp.einsum('tjih,rjh->tjir', queries, prompt_keys) * QUERY_SCALE
    prefix_ok = (jnp.arange(PLEN) < limit)[None, None, None, :]
    prefix = jnp.where(prefix_ok, prefix, NEG_FILL)
    own = jnp.einsum('tjih,ujh->tjiu', queries, key_rows) * QUERY_SCALE
    causal = (jnp.arange(CLEN)[None, :] <= jnp.arange(CLEN)[:, None])[:, None, None, :]
    own = jnp.where(causal, own, NEG_FILL)
    row_max = jnp.maximum(lax.optimization_barrier(jnp.max(prefix, axis=-1)), lax.optimization_barrier(jnp.max(own, axis=-1)))
    prefix_weights = jnp.where(prefix_ok, jnp.exp(prefix - row_max[..., None]), 0.0)
    own_weights = jnp.where(causal, jnp.exp(own - row_max[..., None]), 0.0)
    totals = lax.optimization_barrier(jnp.sum(prefix_weights, axis=-1)) + lax.optimization_barrier(jnp.sum(own_weights, axis=-1))
    prefix_b = prefix_weights.astype(jnp.bfloat16).astype(jnp.float32)
    own_b = own_weights.astype(jnp.bfloat16).astype(jnp.float32)
    numerator = jnp.einsum('tjir,rjh->tjih', prefix_b, prompt_values)
    numerator = numerator + jnp.einsum('tjiu,ujh->tjih', own_b, value_rows)
    attended = (numerator / totals[..., None]).astype(jnp.bfloat16).reshape(CLEN, H * HD)
    span = H * HD // N_SEQ
    projected = jnp.zeros((CLEN, D), jnp.float32)
    for shard in range(N_SEQ):
        partial_sum = jnp.dot(attended[:, shard * span:(shard + 1) * span].astype(jnp.float32), out_weight[shard * span:(shard + 1) * span].astype(jnp.float32), preferred_element_type=jnp.float32)
        rounded = lax.optimization_barrier(partial_sum.astype(jnp.bfloat16))
        projected = projected + rounded.astype(jnp.float32)
    spread = lax.rsqrt(lax.optimization_barrier(jnp.mean(projected * projected, axis=-1, keepdims=True)) + NORM_EPS)
    normed = projected * spread * post_gain
    return (residual.astype(jnp.float32) + normed).astype(jnp.bfloat16)

def reference(residual, cand_qkv, prompt_kv, prompt_len, cand_prompt, out_weight, post_gain):

    def one_candidate(packed):
        return score_one(packed[0], packed[1], packed[2], prompt_kv, prompt_len, out_weight, post_gain)
    return lax.map(one_candidate, (residual, cand_qkv, cand_prompt))
```

```python
import functools
import math

import jax
import jax.numpy as jnp
from jax import lax
from jax.experimental import pallas as pl
from jax.experimental.pallas import tpu as pltpu
from jax.sharding import Mesh, PartitionSpec as P

QUERY_SCALE = 144.0 ** (-0.5)
EXP2_SCALE = QUERY_SCALE / math.log(2.0)
NORM_EPS = 1e-06
NEG_FILL = -1e30
GROUP = ("x", "yl", "core")
SEQ = ("z", "yh")
MIB = 1 << 20


def pick_kernel(order_ref, src_ref, dst_ref, sems):
    count = dst_ref.shape[0]
    copies = [
        pltpu.make_async_copy(src_ref.at[order_ref[i]], dst_ref.at[i], sems.at[i])
        for i in range(count)
    ]
    for copy in copies:
        copy.start()
    for copy in copies:
        copy.wait()


def pick(order, rows):
    return pl.pallas_call(
        pick_kernel,
        out_shape=jax.ShapeDtypeStruct(rows.shape, rows.dtype),
        in_specs=[
            pl.BlockSpec(memory_space=pltpu.SMEM),
            pl.BlockSpec(memory_space=pl.ANY),
        ],
        out_specs=pl.BlockSpec(memory_space=pl.ANY),
        scratch_shapes=[pltpu.SemaphoreType.DMA((rows.shape[0],))],
        name="pick_prompts",
    )(order, rows)


def attend_kernel(limit_ref, qkv_ref, kv_ref, out_ref, own_v, prompt_v, *, block):
    tokens = qkv_ref.shape[0]
    places = kv_ref.shape[0]
    hd = 128
    dims = (((1,), (1,)), ((), ()))
    own_v[:, :hd] = qkv_ref[:, 3 * hd :]
    own_v[:, hd:] = jnp.ones((tokens, hd), jnp.bfloat16)
    prompt_v[:, :hd] = kv_ref[:, hd:]
    prompt_v[:, hd:] = jnp.ones((places, hd), jnp.bfloat16)
    limit = limit_ref[0]
    prompt_bias = jnp.where(
        lax.broadcasted_iota(jnp.int32, (1, places), 1) < limit, 0.0, NEG_FILL
    ).astype(jnp.float32)
    rows = lax.broadcasted_iota(jnp.int32, (block, block), 0)
    cols = lax.broadcasted_iota(jnp.int32, (block, block), 1)
    tri = jnp.where(cols <= rows, 0.0, NEG_FILL).astype(jnp.float32)
    tri = jnp.concatenate([tri, tri], axis=0)
    for b in range(tokens // block):
        at = slice(b * block, (b + 1) * block)
        q = jnp.concatenate([qkv_ref[at, :hd], qkv_ref[at, hd : 2 * hd]], axis=0)
        score = functools.partial(
            lax.dot_general, q, dimension_numbers=dims, preferred_element_type=jnp.float32
        )
        pieces = [score(kv_ref[:, :hd]) + prompt_bias]
        values = [prompt_v[...]]
        if b > 0:
            pieces.append(score(qkv_ref[: b * block, 2 * hd : 3 * hd]))
            values.append(own_v[: b * block, :])
        pieces.append(score(qkv_ref[at, 2 * hd : 3 * hd]) + tri)
        values.append(own_v[at, :])
        top = functools.reduce(
            jnp.maximum, [jnp.max(s, axis=-1, keepdims=True) for s in pieces]
        )
        total = None
        for s, v in zip(pieces, values):
            w = jnp.exp2((s - top) * EXP2_SCALE).astype(jnp.bfloat16)
            part = jnp.dot(w, v, preferred_element_type=jnp.float32)
            total = part if total is None else total + part
        done = (total[:, :hd] / total[:, hd:]).astype(jnp.bfloat16)
        out_ref[at, :hd] = done[:block]
        out_ref[at, hd:] = done[block:]


def attend(limit, qkv, kv, block=256):
    tokens, places = qkv.shape[0], kv.shape[0]
    vmem = pl.BlockSpec(memory_space=pltpu.VMEM)
    return pl.pallas_call(
        functools.partial(attend_kernel, block=block),
        out_shape=jax.ShapeDtypeStruct((tokens, 256), jnp.bfloat16),
        in_specs=[pl.BlockSpec(memory_space=pltpu.SMEM), vmem, vmem],
        out_specs=vmem,
        scratch_shapes=[
            pltpu.VMEM((tokens, 256), jnp.bfloat16),
            pltpu.VMEM((places, 256), jnp.bfloat16),
        ],
        compiler_params=pltpu.CompilerParams(vmem_limit_bytes=40 * MIB),
        cost_estimate=pl.CostEstimate(
            flops=8 * 10**9, bytes_accessed=3 * MIB, transcendentals=6 * 10**6
        ),
        name="attend",
    )(limit, qkv, kv)


def project_kernel(spot_ref, own_ref, other_ref, w0, w1, w2, w3, send_ref, keep_ref, wbuf, sems):
    quarter = w0.shape[1]
    copies = []
    for i, w in enumerate((w0, w1, w2, w3)):
        at = pl.multiple_of(spot_ref[i] * quarter, quarter)
        copies.append(pltpu.make_async_copy(w, wbuf.at[:, pl.ds(at, quarter), :], sems.at[i]))
    for copy in copies:
        copy.start()
    blocks, half = own_ref.shape[0], own_ref.shape[1] // 2
    here = pl.multiple_of(spot_ref[4] * half, half)
    there = pl.multiple_of((1 - spot_ref[4]) * half, half)

    def stack(at):
        return [
            jnp.concatenate([own_ref[n, pl.ds(at, half), :], other_ref[n, pl.ds(at, half), :]], axis=0)
            for n in range(blocks)
        ]

    rows = [jnp.concatenate([a, b], axis=0) for a, b in zip(stack(there), stack(here))]
    for copy in copies:
        copy.wait()
    width = 256
    for j in range(wbuf.shape[2] // width):
        at = slice(j * width, (j + 1) * width)
        total = None
        for n in range(blocks):
            part = jnp.dot(rows[n], wbuf[n, :, at], preferred_element_type=jnp.float32)
            total = part if total is None else total + part
        send_ref[:, at] = total[: 2 * half].astype(jnp.bfloat16)
        keep_ref[:, at] = total[2 * half :]


def project(spots, own, other, weights):
    vmem = pl.BlockSpec(memory_space=pltpu.VMEM)
    blocks, quarter, cols = weights[0].shape
    tokens = own.shape[1]
    return pl.pallas_call(
        project_kernel,
        out_shape=(
            jax.ShapeDtypeStruct((tokens, cols), jnp.bfloat16),
            jax.ShapeDtypeStruct((tokens, cols), jnp.float32),
        ),
        in_specs=[pl.BlockSpec(memory_space=pltpu.SMEM), vmem, vmem]
        + [pl.BlockSpec(memory_space=pl.ANY)] * 4,
        out_specs=(vmem, vmem),
        scratch_shapes=[
            pltpu.VMEM((blocks, 4 * quarter, cols), jnp.bfloat16),
            pltpu.SemaphoreType.DMA((4,)),
        ],
        compiler_params=pltpu.CompilerParams(vmem_limit_bytes=40 * MIB),
        cost_estimate=pl.CostEstimate(
            flops=2 * 2 * tokens * blocks * 4 * quarter * cols,
            bytes_accessed=12 * MIB,
            transcendentals=0,
        ),
        name="project",
    )(spots, own, other, *weights)


def body(residual, cand_qkv, prompt_kv, prompt_len, cand_prompt, out_weight, post_gain):
    x, yl, core = (lax.axis_index(n) for n in GROUP)
    yh = lax.axis_index("yh")
    nx, nz = lax.axis_size("x"), lax.axis_size("z")
    group = lax.axis_index(GROUP)
    per_device, heads, width = cand_qkv.shape[1:]
    features = residual.shape[-1]
    half_cols = features // 2
    rows_here = out_weight.shape[0]
    quarter = rows_here // 4

    color = (x + 2 * yl) % 4
    piece = lax.dynamic_slice(
        out_weight, (color * quarter, core * half_cols), (quarter, half_cols)
    )
    w_own = lax.all_gather(piece, "z", axis=0, tiled=False)

    prompts = lax.all_to_all(
        pick(cand_prompt, prompt_kv.reshape(prompt_kv.shape[0], prompt_kv.shape[1], -1)),
        GROUP, 0, 0, tiled=True,
    )
    prompts = prompts.reshape(-1, prompts.shape[-1])
    by_head = cand_qkv[0].transpose(1, 0, 2)
    by_head, prompts = lax.optimization_barrier((by_head, prompts))
    qkv = lax.all_to_all(by_head, SEQ, 0, 0, tiled=True).reshape(-1, width)
    qkv, w_own = lax.optimization_barrier((qkv, w_own))

    up = [(i, (i + 1) % nx) for i in range(nx)]
    down = [(i, (i - 1) % nx) for i in range(nx)]
    swap = [(0, 1), (1, 0)]
    w_left = lax.ppermute(w_own, "x", up)
    w_right = lax.ppermute(w_own, "x", down)
    w_side = lax.ppermute(w_own, "yl", swap)

    limit = prompt_len[cand_prompt[group]].reshape(1)
    attended = attend(limit, qkv, prompts)

    own = lax.all_to_all(
        attended.reshape(nz, -1, attended.shape[-1]), "z", 0, 0, tiled=True
    )
    other = lax.ppermute(own, "core", swap)
    spots = jnp.stack([color, (color + 3) % 4, (color + 1) % 4, (color + 2) % 4, yh]).astype(jnp.int32)
    send, keep = project(spots, own, other, (w_own, w_left, w_right, w_side))
    summed = lax.ppermute(send, "yh", swap).astype(jnp.float32) + keep
    mine, theirs = summed[:per_device], summed[per_device:]
    back = lax.ppermute(theirs.astype(jnp.bfloat16), "core", swap).astype(jnp.float32)
    first = core == 0
    projected = jnp.concatenate(
        [jnp.where(first, mine, back), jnp.where(first, back, mine)], axis=1
    )
    spread = lax.rsqrt(jnp.mean(projected * projected, axis=-1, keepdims=True) + NORM_EPS)
    normed = projected * spread * post_gain
    return (residual.astype(jnp.float32) + normed[None]).astype(jnp.bfloat16)


def solution(mesh):
    fine = Mesh(mesh.devices.reshape(4, 2, 2, 8, 2), GROUP + SEQ)
    return jax.shard_map(
        body,
        mesh=fine,
        in_specs=(
            P(GROUP, SEQ, None),
            P(GROUP, SEQ, None, None),
            P(None, GROUP, SEQ, None),
            P(),
            P(),
            P(SEQ, None),
            P(),
        ),
        out_specs=P(GROUP, SEQ, None),
        check_vma=False,
    )
```

```python
import functools
import math

import jax
import jax.numpy as jnp
from jax import lax
from jax.experimental import pallas as pl
from jax.experimental.pallas import tpu as pltpu
from jax.sharding import Mesh, PartitionSpec as P

QUERY_SCALE = 144.0 ** (-0.5)
EXP2_SCALE = QUERY_SCALE / math.log(2.0)
NORM_EPS = 1e-06
NEG_FILL = -1e30
GROUP = ("x", "yl", "core")
SEQ = ("z", "yh")
MIB = 1 << 20
BLOCK_LOTS = ((0, 1, -1, 2, -2, 3, -3, 4),)


def pick_kernel(order_ref, src_ref, dst_ref, sems):
    count = dst_ref.shape[0]
    copies = [
        pltpu.make_async_copy(src_ref.at[order_ref[i]], dst_ref.at[i], sems.at[i])
        for i in range(count)
    ]
    for copy in copies:
        copy.start()
    for copy in copies:
        copy.wait()


def pick(order, rows):
    return pl.pallas_call(
        pick_kernel,
        out_shape=jax.ShapeDtypeStruct(rows.shape, rows.dtype),
        in_specs=[
            pl.BlockSpec(memory_space=pltpu.SMEM),
            pl.BlockSpec(memory_space=pl.ANY),
        ],
        out_specs=pl.BlockSpec(memory_space=pltpu.VMEM),
        scratch_shapes=[pltpu.SemaphoreType.DMA((rows.shape[0],))],
        name="pick_prompts",
    )(order, rows)


def attend_kernel(spot_ref, order_ref, length_ref, qkv_ref, kv_ref, out_ref, own_v, prompt_v, *, block):
    tokens = qkv_ref.shape[0]
    places = kv_ref.shape[0]
    hd = 128
    dims = (((1,), (1,)), ((), ()))
    own_v[:, :hd] = qkv_ref[:, 3 * hd :]
    own_v[:, hd:] = jnp.ones((tokens, hd), jnp.bfloat16)
    prompt_v[:, :hd] = kv_ref[:, hd:]
    prompt_v[:, hd:] = jnp.ones((places, hd), jnp.bfloat16)
    limit = length_ref[order_ref[spot_ref[0]]]
    prompt_bias = jnp.where(
        lax.broadcasted_iota(jnp.int32, (1, places), 1) < limit, 0.0, NEG_FILL
    ).astype(jnp.float32)
    rows = lax.broadcasted_iota(jnp.int32, (block, block), 0)
    cols = lax.broadcasted_iota(jnp.int32, (block, block), 1)
    tri = jnp.where(cols <= rows, 0.0, NEG_FILL).astype(jnp.float32)
    tri = jnp.concatenate([tri, tri], axis=0)
    for b in range(tokens // block):
        at = slice(b * block, (b + 1) * block)
        q = jnp.concatenate([qkv_ref[at, :hd], qkv_ref[at, hd : 2 * hd]], axis=0)
        score = functools.partial(
            lax.dot_general, q, dimension_numbers=dims, preferred_element_type=jnp.float32
        )
        pieces = [score(kv_ref[:, :hd]) + prompt_bias]
        values = [prompt_v[...]]
        if b > 0:
            pieces.append(score(qkv_ref[: b * block, 2 * hd : 3 * hd]))
            values.append(own_v[: b * block, :])
        pieces.append(score(qkv_ref[at, 2 * hd : 3 * hd]) + tri)
        values.append(own_v[at, :])
        top = functools.reduce(
            jnp.maximum, [jnp.max(s, axis=-1, keepdims=True) for s in pieces]
        )
        total = None
        for s, v in zip(pieces, values):
            w = jnp.exp2((s - top) * EXP2_SCALE).astype(jnp.bfloat16)
            part = jnp.dot(w, v, preferred_element_type=jnp.float32)
            total = part if total is None else total + part
        done = total[:, :hd] / total[:, hd:]
        done = jnp.concatenate([done[:block], done[block:]], axis=1)
        out_ref[at, :] = pltpu.roll(done, spot_ref[1], 1).astype(jnp.bfloat16)


def attend(spots, order, lengths, qkv, kv, block=256):
    tokens, places = qkv.shape[0], kv.shape[0]
    vmem = pl.BlockSpec(memory_space=pltpu.VMEM)
    return pl.pallas_call(
        functools.partial(attend_kernel, block=block),
        out_shape=jax.ShapeDtypeStruct((tokens, 256), jnp.bfloat16),
        in_specs=[pl.BlockSpec(memory_space=pltpu.SMEM)] * 3 + [vmem, vmem],
        out_specs=vmem,
        scratch_shapes=[
            pltpu.VMEM((tokens, 256), jnp.bfloat16),
            pltpu.VMEM((places, 256), jnp.bfloat16),
        ],
        compiler_params=pltpu.CompilerParams(vmem_limit_bytes=32 * MIB),
        cost_estimate=pl.CostEstimate(
            flops=10**6, bytes_accessed=MIB // 16, transcendentals=0
        ),
        name="attend",
    )(spots, order, lengths, qkv, kv)


def project_kernel(spot_ref, own_ref, other_ref, *refs):
    weights, (send_ref, keep_ref, total) = refs[:-3], refs[-3:]
    blocks = own_ref.shape[0]
    cols = keep_ref.shape[1]
    half = own_ref.shape[1] // 2
    here = pl.multiple_of(spot_ref[0] * half, half)
    there = pl.multiple_of((1 - spot_ref[0]) * half, half)
    width = 256
    places = [(lot, k) for lot in range(len(weights) // 4) for k in range(weights[4 * lot].shape[0])]
    for r, (lot, k) in enumerate(places):
        n = lax.rem(spot_ref[1] + BLOCK_LOTS[lot][k] + blocks, blocks)
        tokens = jnp.concatenate(
            [ref[n, pl.ds(at, half), :] for at in (there, here) for ref in (own_ref, other_ref)],
            axis=0,
        )
        for j in range(cols // width):
            at = slice(j * width, (j + 1) * width)
            block = jnp.concatenate([weights[4 * lot + i][k, :, at] for i in range(4)], axis=0)
            part = jnp.dot(tokens, block, preferred_element_type=jnp.float32)
            if r > 0:
                part = part + total[:, at]
            if r < blocks - 1:
                total[:, at] = part
            else:
                send_ref[:, at] = part[: 2 * half].astype(jnp.bfloat16)
                keep_ref[:, at] = part[2 * half :]


def project(spots, own, other, weights):
    vmem = pl.BlockSpec(memory_space=pltpu.VMEM)
    quarter, cols = weights[0].shape[1:]
    blocks, tokens = own.shape[:2]
    return pl.pallas_call(
        project_kernel,
        out_shape=(
            jax.ShapeDtypeStruct((tokens, cols), jnp.bfloat16),
            jax.ShapeDtypeStruct((tokens, cols), jnp.float32),
        ),
        in_specs=[pl.BlockSpec(memory_space=pltpu.SMEM)] + [vmem] * (2 + len(weights)),
        out_specs=(vmem, vmem),
        scratch_shapes=[pltpu.VMEM((2 * tokens, cols), jnp.float32)],
        compiler_params=pltpu.CompilerParams(vmem_limit_bytes=32 * MIB),
        cost_estimate=pl.CostEstimate(
            flops=2 * 2 * tokens * blocks * 4 * quarter * cols,
            bytes_accessed=12 * MIB,
            transcendentals=0,
        ),
        name="project",
    )(spots, own, other, *weights)


def body(residual, cand_qkv, prompt_kv, prompt_len, cand_prompt, out_weight, post_gain):
    x, yl, core = (lax.axis_index(n) for n in GROUP)
    yh = lax.axis_index("yh")
    nx, nz = lax.axis_size("x"), lax.axis_size("z")
    group = lax.axis_index(GROUP)
    per_device, heads, width = cand_qkv.shape[1:]
    features = residual.shape[-1]
    half_cols = features // 2
    rows_here = out_weight.shape[0]
    quarter = rows_here // 4

    color = (x + 2 * yl) % 4
    piece = lax.dynamic_slice(
        out_weight, (color * quarter, core * half_cols), (quarter, half_cols)
    )
    def from_z(block, distance):
        return lax.ppermute(block, "z", [((i + distance) % nz, i) for i in range(nz)])

    def from_sides(lot):
        return [
            lot,
            lax.ppermute(lot, "x", [(i, (i - 1) % nx) for i in range(nx)]),
            lax.ppermute(lot, "yl", swap),
            lax.ppermute(lot, "x", [(i, (i + 1) % nx) for i in range(nx)]),
        ]

    swap = [(0, 1), (1, 0)]
    blocks = {0: piece, **{d: from_z(piece, d) for d in (1, -1, 2, -2)}}
    blocks.update({3: from_z(blocks[2], 1), -3: from_z(blocks[-2], -1)})
    blocks[4] = from_z(blocks[3], 1)
    lots = [jnp.stack([blocks[d] for d in lot]) for lot in BLOCK_LOTS]
    picked = pick(cand_prompt, prompt_kv.reshape(prompt_kv.shape[0], prompt_kv.shape[1], -1))
    prompts = lax.all_to_all(picked, GROUP, 0, 0, tiled=True)
    prompts = prompts.reshape(-1, prompts.shape[-1])
    by_head = cand_qkv[0].transpose(1, 0, 2)
    by_head, prompts, lots = lax.optimization_barrier((by_head, prompts, lots))
    qkv = lax.all_to_all(by_head, SEQ, 0, 0, tiled=True).reshape(-1, width)
    weights = from_sides(lots[0])

    turn = (4 - color) % 4 * quarter
    attended = attend(
        jnp.stack([group, turn]).astype(jnp.int32), cand_prompt, prompt_len, qkv, prompts
    )
    own = lax.all_to_all(
        attended.reshape(nz, -1, attended.shape[-1]), "z", 0, 0, tiled=True
    )
    other = lax.ppermute(own, "core", swap)
    spots = jnp.stack([yh, lax.axis_index("z")]).astype(jnp.int32)
    send, keep = project(spots, own, other, weights)
    summed = lax.ppermute(send, "yh", swap).astype(jnp.float32) + keep
    mine, theirs = summed[:per_device], summed[per_device:]
    back = lax.ppermute(theirs.astype(jnp.bfloat16), "core", swap).astype(jnp.float32)
    first = core == 0
    projected = jnp.concatenate(
        [jnp.where(first, mine, back), jnp.where(first, back, mine)], axis=1
    )
    spread = lax.rsqrt(jnp.mean(projected * projected, axis=-1, keepdims=True) + NORM_EPS)
    normed = projected * spread * post_gain
    return (residual.astype(jnp.float32) + normed[None]).astype(jnp.bfloat16)


def solution(mesh):
    fine = Mesh(mesh.devices.reshape(4, 2, 2, 8, 2), GROUP + SEQ)
    return jax.shard_map(
        body,
        mesh=fine,
        in_specs=(
            P(GROUP, SEQ, None),
            P(GROUP, SEQ, None, None),
            P(None, GROUP, SEQ, None),
            P(),
            P(),
            P(SEQ, None),
            P(),
        ),
        out_specs=P(GROUP, SEQ, None),
        check_vma=False,
    )
```

```python
import functools
import math

import jax
import jax.numpy as jnp
from jax import lax
from jax.experimental import pallas as pl
from jax.experimental.pallas import tpu as pltpu
from jax.sharding import Mesh, PartitionSpec as P

QUERY_SCALE = 144.0 ** (-0.5)
EXP2_SCALE = QUERY_SCALE / math.log(2.0)
NORM_EPS = 1e-06
NEG_FILL = -1e30
GROUP = ("x", "yl", "core")
SEQ = ("z", "yh")
MIB = 1 << 20
BLOCK_LOTS = ((0, 1, -1, 2, -2, 3, -3), (4,))


def prepare_kernel(order_ref, corner_ref, kv_ref, weight_ref, picked_ref, piece_ref, sems):
    count = picked_ref.shape[0]
    rows, cols = piece_ref.shape
    top = pl.multiple_of(corner_ref[0] * rows, rows)
    left = pl.multiple_of(corner_ref[1] * cols, cols)
    copies = [
        pltpu.make_async_copy(
            weight_ref.at[pl.ds(top, rows), pl.ds(left, cols)], piece_ref, sems.at[count]
        )
    ]
    for i in range(count):
        copies.append(
            pltpu.make_async_copy(kv_ref.at[order_ref[i]], picked_ref.at[i], sems.at[i])
        )
    for copy in copies:
        copy.start()
    for copy in copies:
        copy.wait()


def prepare(order, corner, kv, weight, rows, cols):
    smem = pl.BlockSpec(memory_space=pltpu.SMEM)
    vmem = pl.BlockSpec(memory_space=pltpu.VMEM)
    whole = pl.BlockSpec(memory_space=pltpu.HBM)
    return pl.pallas_call(
        prepare_kernel,
        out_shape=(
            jax.ShapeDtypeStruct(kv.shape, kv.dtype),
            jax.ShapeDtypeStruct((rows, cols), weight.dtype),
        ),
        in_specs=[smem, smem, whole, whole],
        out_specs=(vmem, vmem),
        scratch_shapes=[pltpu.SemaphoreType.DMA((kv.shape[0] + 1,))],
        name="prepare",
    )(order, corner, kv, weight)


def attend_kernel(spot_ref, order_ref, length_ref, qkv_ref, kv_ref, out_ref, own_v, prompt_v, *, block, chunk):
    tokens = qkv_ref.shape[0]
    places = kv_ref.shape[0]
    hd = 128
    dims = (((1,), (1,)), ((), ()))
    own_v[:, :hd] = qkv_ref[:, 3 * hd :]
    own_v[:, hd:] = jnp.ones((tokens, hd), jnp.bfloat16)
    prompt_v[:, :hd] = kv_ref[:, hd:]
    prompt_v[:, hd:] = jnp.ones((places, hd), jnp.bfloat16)
    limit = length_ref[order_ref[spot_ref[0]]]
    prompt_bias = jnp.where(
        lax.broadcasted_iota(jnp.int32, (1, places), 1) < limit, 0.0, NEG_FILL
    ).astype(jnp.float32)
    rows = lax.broadcasted_iota(jnp.int32, (block, block), 0)
    cols = lax.broadcasted_iota(jnp.int32, (block, block), 1)
    tri = jnp.where(cols <= rows, 0.0, NEG_FILL).astype(jnp.float32)
    tri = jnp.concatenate([tri, tri], axis=0)

    def scores(b):
        at = slice(b * block, (b + 1) * block)
        q = jnp.concatenate([qkv_ref[at, :hd], qkv_ref[at, hd : 2 * hd]], axis=0)
        score = functools.partial(
            lax.dot_general, q, dimension_numbers=dims, preferred_element_type=jnp.float32
        )
        pieces, values = [], []
        for c in range(0, places, chunk):
            part = slice(c, c + chunk)
            pieces.append(score(kv_ref[part, :hd]) + prompt_bias[:, part])
            values.append(prompt_v[part, :])
        if b > 0:
            pieces.append(score(qkv_ref[: b * block, 2 * hd : 3 * hd]))
            values.append(own_v[: b * block, :])
        pieces.append(score(qkv_ref[at, 2 * hd : 3 * hd]) + tri)
        values.append(own_v[at, :])
        return pieces, values

    def finish(b, pieces, values):
        at = slice(b * block, (b + 1) * block)
        top = functools.reduce(
            jnp.maximum, [jnp.max(s, axis=-1, keepdims=True) for s in pieces]
        )
        total = None
        for s, v in zip(pieces, values):
            w = jnp.exp2((s - top) * EXP2_SCALE).astype(jnp.bfloat16)
            part = jnp.dot(w, v, preferred_element_type=jnp.float32)
            total = part if total is None else total + part
        done = total[:, :hd] / total[:, hd:]
        done = jnp.concatenate([done[:block], done[block:]], axis=1)
        out_ref[at, :] = pltpu.roll(done, spot_ref[1], 1).astype(jnp.bfloat16)

    count = tokens // block
    coming = scores(0)
    for b in range(count):
        current = coming
        if b + 1 < count:
            coming = scores(b + 1)
        finish(b, *current)


def attend(spots, order, lengths, qkv, kv, block=256, chunk=512):
    tokens, places = qkv.shape[0], kv.shape[0]
    vmem = pl.BlockSpec(memory_space=pltpu.VMEM)
    return pl.pallas_call(
        functools.partial(attend_kernel, block=block, chunk=chunk),
        out_shape=jax.ShapeDtypeStruct((tokens, 256), jnp.bfloat16),
        in_specs=[pl.BlockSpec(memory_space=pltpu.SMEM)] * 3 + [vmem, vmem],
        out_specs=vmem,
        scratch_shapes=[
            pltpu.VMEM((tokens, 256), jnp.bfloat16),
            pltpu.VMEM((places, 256), jnp.bfloat16),
        ],
        compiler_params=pltpu.CompilerParams(vmem_limit_bytes=32 * MIB),
        cost_estimate=pl.CostEstimate(
            flops=10**6, bytes_accessed=MIB // 16, transcendentals=0
        ),
        name="attend",
    )(spots, order, lengths, qkv, kv)


def project_kernel(spot_ref, own_ref, other_ref, *refs):
    weights, (send_ref, keep_ref, total) = refs[:-3], refs[-3:]
    blocks = own_ref.shape[0]
    cols = keep_ref.shape[1]
    half = own_ref.shape[1] // 2
    here = pl.multiple_of(spot_ref[0] * half, half)
    there = pl.multiple_of((1 - spot_ref[0]) * half, half)
    width = 256
    places = [(lot, k) for lot in range(len(weights) // 4) for k in range(weights[4 * lot].shape[0])]
    for r, (lot, k) in enumerate(places):
        n = lax.rem(spot_ref[1] + BLOCK_LOTS[lot][k] + blocks, blocks)
        tokens = jnp.concatenate(
            [ref[n, pl.ds(at, half), :] for at in (there, here) for ref in (own_ref, other_ref)],
            axis=0,
        )
        for j in range(cols // width):
            at = slice(j * width, (j + 1) * width)
            block = jnp.concatenate([weights[4 * lot + i][k, :, at] for i in range(4)], axis=0)
            part = jnp.dot(tokens, block, preferred_element_type=jnp.float32)
            if r > 0:
                part = part + total[:, at]
            if r < blocks - 1:
                total[:, at] = part
            else:
                send_ref[:, at] = part[: 2 * half].astype(jnp.bfloat16)
                keep_ref[:, at] = part[2 * half :]


def project(spots, own, other, weights):
    vmem = pl.BlockSpec(memory_space=pltpu.VMEM)
    quarter, cols = weights[0].shape[1:]
    blocks, tokens = own.shape[:2]
    return pl.pallas_call(
        project_kernel,
        out_shape=(
            jax.ShapeDtypeStruct((tokens, cols), jnp.bfloat16),
            jax.ShapeDtypeStruct((tokens, cols), jnp.float32),
        ),
        in_specs=[pl.BlockSpec(memory_space=pltpu.SMEM)] + [vmem] * (2 + len(weights)),
        out_specs=(vmem, vmem),
        scratch_shapes=[pltpu.VMEM((2 * tokens, cols), jnp.float32)],
        compiler_params=pltpu.CompilerParams(vmem_limit_bytes=32 * MIB),
        cost_estimate=pl.CostEstimate(
            flops=2 * 2 * tokens * blocks * 4 * quarter * cols,
            bytes_accessed=12 * MIB,
            transcendentals=0,
        ),
        name="project",
    )(spots, own, other, *weights)


def body(residual, cand_qkv, prompt_kv, prompt_len, cand_prompt, out_weight, post_gain):
    x, yl, core = (lax.axis_index(n) for n in GROUP)
    yh = lax.axis_index("yh")
    nx, nz = lax.axis_size("x"), lax.axis_size("z")
    group = lax.axis_index(GROUP)
    per_device, heads, width = cand_qkv.shape[1:]
    features = residual.shape[-1]
    half_cols = features // 2
    rows_here = out_weight.shape[0]
    quarter = rows_here // 4

    color = (x + 2 * yl) % 4
    picked, piece = prepare(
        cand_prompt,
        jnp.stack([color, core]).astype(jnp.int32),
        prompt_kv.reshape(prompt_kv.shape[0], prompt_kv.shape[1], -1),
        out_weight,
        quarter,
        half_cols,
    )
    def from_z(block, distance):
        return lax.ppermute(block, "z", [((i + distance) % nz, i) for i in range(nz)])

    def from_sides(lot):
        return [
            lot,
            lax.ppermute(lot, "x", [(i, (i - 1) % nx) for i in range(nx)]),
            lax.ppermute(lot, "yl", swap),
            lax.ppermute(lot, "x", [(i, (i + 1) % nx) for i in range(nx)]),
        ]

    swap = [(0, 1), (1, 0)]
    blocks = {0: piece, **{d: from_z(piece, d) for d in (1, -1, 2, -2)}}
    blocks.update({3: from_z(blocks[2], 1), -3: from_z(blocks[-2], -1)})
    near = jnp.stack([blocks[d] for d in BLOCK_LOTS[0]])
    prompts = lax.all_to_all(picked, GROUP, 0, 0, tiled=True)
    prompts = prompts.reshape(-1, prompts.shape[-1])
    by_head = cand_qkv[0].transpose(1, 0, 2)
    by_head, prompts, near = lax.optimization_barrier((by_head, prompts, near))
    qkv = lax.all_to_all(by_head, SEQ, 0, 0, tiled=True).reshape(-1, width)
    weights = from_sides(near)
    qkv, block = lax.optimization_barrier((qkv, blocks[3]))
    block = from_z(block, 1)

    turn = (4 - color) % 4 * quarter
    attended = attend(
        jnp.stack([group, turn]).astype(jnp.int32), cand_prompt, prompt_len, qkv, prompts
    )
    attended, block = lax.optimization_barrier((attended, block))
    own = lax.all_to_all(
        attended.reshape(nz, -1, attended.shape[-1]), "z", 0, 0, tiled=True
    )
    own, last = lax.optimization_barrier((own, from_sides(block[None])))
    other = lax.ppermute(own, "core", swap)
    spots = jnp.stack([yh, lax.axis_index("z")]).astype(jnp.int32)
    send, keep = project(spots, own, other, weights + last)
    summed = lax.ppermute(send, "yh", swap).astype(jnp.float32) + keep
    mine, theirs = summed[:per_device], summed[per_device:]
    back = lax.ppermute(theirs.astype(jnp.bfloat16), "core", swap).astype(jnp.float32)
    first = core == 0
    projected = jnp.concatenate(
        [jnp.where(first, mine, back), jnp.where(first, back, mine)], axis=1
    )
    spread = lax.rsqrt(jnp.mean(projected * projected, axis=-1, keepdims=True) + NORM_EPS)
    normed = projected * spread * post_gain
    return (residual.astype(jnp.float32) + normed[None]).astype(jnp.bfloat16)


def solution(mesh):
    fine = Mesh(mesh.devices.reshape(4, 2, 2, 8, 2), GROUP + SEQ)
    return jax.shard_map(
        body,
        mesh=fine,
        in_specs=(
            P(GROUP, SEQ, None),
            P(GROUP, SEQ, None, None),
            P(None, GROUP, SEQ, None),
            P(),
            P(),
            P(SEQ, None),
            P(),
        ),
        out_specs=P(GROUP, SEQ, None),
        check_vma=False,
    )
```

```python
import functools
import math

import jax
import jax.numpy as jnp
from jax import lax
from jax.experimental import pallas as pl
from jax.experimental.pallas import tpu as pltpu
from jax.sharding import Mesh, PartitionSpec as P

QUERY_SCALE = 144.0 ** (-0.5)
EXP2_SCALE = QUERY_SCALE / math.log(2.0)
NORM_EPS = 1e-06
NEG_FILL = -1e30
GROUP = ("x", "yl", "core")
SEQ = ("z", "yh")
MIB = 1 << 20
BLOCK_LOTS = ((1, -1, 2, -2, 3, -3), (4,))


def prepare_kernel(order_ref, kv_ref, weight_ref, picked_ref, piece_ref, sems):
    count = picked_ref.shape[0]
    rows, cols = piece_ref.shape
    color = (lax.axis_index("x") + 2 * lax.axis_index("yl")) % 4
    top = pl.multiple_of(color * rows, rows)
    left = pl.multiple_of(lax.axis_index("core") * cols, cols)
    copies = [
        pltpu.make_async_copy(
            weight_ref.at[pl.ds(top, rows), pl.ds(left, cols)], piece_ref, sems.at[count]
        )
    ]
    for i in range(count):
        copies.append(
            pltpu.make_async_copy(kv_ref.at[order_ref[i]], picked_ref.at[i], sems.at[i])
        )
    for copy in copies:
        copy.start()
    for copy in copies:
        copy.wait()


def prepare(order, kv, weight, rows, cols):
    smem = pl.BlockSpec(memory_space=pltpu.SMEM)
    vmem = pl.BlockSpec(memory_space=pltpu.VMEM)
    whole = pl.BlockSpec(memory_space=pltpu.HBM)
    return pl.pallas_call(
        prepare_kernel,
        out_shape=(
            jax.ShapeDtypeStruct(kv.shape, kv.dtype),
            jax.ShapeDtypeStruct((rows, cols), weight.dtype),
        ),
        in_specs=[smem, whole, whole],
        out_specs=(vmem, vmem),
        scratch_shapes=[pltpu.SemaphoreType.DMA((kv.shape[0] + 1,))],
        name="prepare",
    )(order, kv, weight)


def attend_kernel(spot_ref, order_ref, length_ref, qkv_ref, kv_ref, out_ref, own_v, prompt_v, *, block, chunk):
    tokens = qkv_ref.shape[0]
    places = kv_ref.shape[0]
    hd = 128
    dims = (((1,), (1,)), ((), ()))
    own_v[:, :hd] = qkv_ref[:, 3 * hd :]
    own_v[:, hd:] = jnp.ones((tokens, hd), jnp.bfloat16)
    prompt_v[:, :hd] = kv_ref[:, hd:]
    prompt_v[:, hd:] = jnp.ones((places, hd), jnp.bfloat16)
    limit = length_ref[order_ref[spot_ref[0]]]
    prompt_bias = jnp.where(
        lax.broadcasted_iota(jnp.int32, (1, places), 1) < limit, 0.0, NEG_FILL
    ).astype(jnp.float32)
    rows = lax.broadcasted_iota(jnp.int32, (block, block), 0)
    cols = lax.broadcasted_iota(jnp.int32, (block, block), 1)
    tri = jnp.where(cols <= rows, 0.0, NEG_FILL).astype(jnp.float32)
    tri = jnp.concatenate([tri, tri], axis=0)

    def scores(b):
        at = slice(b * block, (b + 1) * block)
        q = jnp.concatenate([qkv_ref[at, :hd], qkv_ref[at, hd : 2 * hd]], axis=0)
        score = functools.partial(
            lax.dot_general, q, dimension_numbers=dims, preferred_element_type=jnp.float32
        )
        pieces, values = [], []
        for c in range(0, places, chunk):
            part = slice(c, c + chunk)
            pieces.append(score(kv_ref[part, :hd]) + prompt_bias[:, part])
            values.append(prompt_v[part, :])
        if b > 0:
            pieces.append(score(qkv_ref[: b * block, 2 * hd : 3 * hd]))
            values.append(own_v[: b * block, :])
        pieces.append(score(qkv_ref[at, 2 * hd : 3 * hd]) + tri)
        values.append(own_v[at, :])
        return pieces, values

    def finish(b, pieces, values):
        at = slice(b * block, (b + 1) * block)
        top = functools.reduce(
            jnp.maximum, [jnp.max(s, axis=-1, keepdims=True) for s in pieces]
        )
        total = None
        for s, v in zip(pieces, values):
            w = jnp.exp2((s - top) * EXP2_SCALE).astype(jnp.bfloat16)
            part = jnp.dot(w, v, preferred_element_type=jnp.float32)
            total = part if total is None else total + part
        done = total[:, :hd] / total[:, hd:]
        done = jnp.concatenate([done[:block], done[block:]], axis=1)
        out_ref[at, :] = pltpu.roll(done, spot_ref[1], 1).astype(jnp.bfloat16)

    count = tokens // block
    coming = scores(0)
    for b in range(count):
        current = coming
        if b + 1 < count:
            coming = scores(b + 1)
        finish(b, *current)


def attend(spots, order, lengths, qkv, kv, block=256, chunk=512):
    tokens, places = qkv.shape[0], kv.shape[0]
    vmem = pl.BlockSpec(memory_space=pltpu.VMEM)
    return pl.pallas_call(
        functools.partial(attend_kernel, block=block, chunk=chunk),
        out_shape=jax.ShapeDtypeStruct((tokens, 256), jnp.bfloat16),
        in_specs=[pl.BlockSpec(memory_space=pltpu.SMEM)] * 3 + [vmem, vmem],
        out_specs=vmem,
        scratch_shapes=[
            pltpu.VMEM((tokens, 256), jnp.bfloat16),
            pltpu.VMEM((places, 256), jnp.bfloat16),
        ],
        compiler_params=pltpu.CompilerParams(vmem_limit_bytes=32 * MIB),
        cost_estimate=pl.CostEstimate(
            flops=10**6, bytes_accessed=MIB // 16, transcendentals=0
        ),
        name="attend",
    )(spots, order, lengths, qkv, kv)


def project_kernel(spot_ref, own_ref, other_ref, local, *refs):
    weights, (send_ref, keep_ref, total) = refs[:-3], refs[-3:]
    blocks = own_ref.shape[0]
    rows, cols = local.shape
    quarter = rows // 4
    half = own_ref.shape[1] // 2
    here = pl.multiple_of(spot_ref[0] * half, half)
    there = pl.multiple_of((1 - spot_ref[0]) * half, half)
    width = 256
    places = [(d, lot, k) for lot, distances in enumerate(BLOCK_LOTS) for k, d in enumerate(distances)]
    places.append((0, None, None))
    for r, (distance, lot, k) in enumerate(places):
        n = lax.rem(spot_ref[1] + distance + blocks, blocks)
        tokens = jnp.concatenate(
            [ref[n, pl.ds(at, half), :] for at in (there, here) for ref in (own_ref, other_ref)],
            axis=0,
        )
        for j in range(cols // width):
            at = slice(j * width, (j + 1) * width)
            if lot is None:
                quarters = []
                for i in range(4):
                    top = pl.multiple_of(lax.rem(spot_ref[2] + i, 4) * quarter, quarter)
                    quarters.append(local[pl.ds(top, quarter), at])
            else:
                quarters = [weights[4 * lot + i][k, :, at] for i in range(4)]
            part = jnp.dot(
                tokens, jnp.concatenate(quarters, axis=0), preferred_element_type=jnp.float32
            )
            if r > 0:
                part = part + total[:, at]
            if r < blocks - 1:
                total[:, at] = part
            else:
                send_ref[:, at] = part[: 2 * half].astype(jnp.bfloat16)
                keep_ref[:, at] = part[2 * half :]


def project(spots, own, other, local, weights):
    vmem = pl.BlockSpec(memory_space=pltpu.VMEM)
    quarter, cols = weights[0].shape[1:]
    blocks, tokens = own.shape[:2]
    return pl.pallas_call(
        project_kernel,
        out_shape=(
            jax.ShapeDtypeStruct((tokens, cols), jnp.bfloat16),
            jax.ShapeDtypeStruct((tokens, cols), jnp.float32),
        ),
        in_specs=[pl.BlockSpec(memory_space=pltpu.SMEM)] + [vmem] * (3 + len(weights)),
        out_specs=(vmem, vmem),
        scratch_shapes=[
            pltpu.VMEM((2 * tokens, cols), jnp.float32),
        ],
        compiler_params=pltpu.CompilerParams(vmem_limit_bytes=32 * MIB),
        cost_estimate=pl.CostEstimate(
            flops=2 * 2 * tokens * blocks * 4 * quarter * cols,
            bytes_accessed=12 * MIB,
            transcendentals=0,
        ),
        name="project",
    )(spots, own, other, local, *weights)


def body(residual, cand_qkv, prompt_kv, prompt_len, cand_prompt, out_weight, post_gain):
    x, yl, core = (lax.axis_index(n) for n in GROUP)
    yh = lax.axis_index("yh")
    nx, nz = lax.axis_size("x"), lax.axis_size("z")
    group = lax.axis_index(GROUP)
    per_device, heads, width = cand_qkv.shape[1:]
    features = residual.shape[-1]
    half_cols = features // 2
    rows_here = out_weight.shape[0]
    quarter = rows_here // 4

    color = (x + 2 * yl) % 4
    picked, piece = prepare(
        cand_prompt,
        prompt_kv.reshape(prompt_kv.shape[0], prompt_kv.shape[1], -1),
        out_weight,
        quarter,
        half_cols,
    )
    def from_z(block, distance):
        return lax.ppermute(block, "z", [((i + distance) % nz, i) for i in range(nz)])

    def from_sides(lot):
        return [
            lot,
            lax.ppermute(lot, "x", [(i, (i - 1) % nx) for i in range(nx)]),
            lax.ppermute(lot, "yl", swap),
            lax.ppermute(lot, "x", [(i, (i + 1) % nx) for i in range(nx)]),
        ]

    swap = [(0, 1), (1, 0)]
    blocks = {0: piece, **{d: from_z(piece, d) for d in (1, -1, 2, -2)}}
    blocks.update({3: from_z(blocks[2], 1), -3: from_z(blocks[-2], -1)})
    near = jnp.stack([blocks[d] for d in BLOCK_LOTS[0]])
    prompts = lax.all_to_all(picked, GROUP, 0, 0, tiled=True)
    prompts = prompts.reshape(-1, prompts.shape[-1])
    by_head = cand_qkv[0].transpose(1, 0, 2)
    by_head, prompts, near = lax.optimization_barrier((by_head, prompts, near))
    qkv = lax.all_to_all(by_head, SEQ, 0, 0, tiled=True).reshape(-1, width)
    weights = from_sides(near)
    qkv, block = lax.optimization_barrier((qkv, blocks[3]))
    block = from_z(block, 1)

    turn = (4 - color) % 4 * quarter
    attended = attend(
        jnp.stack([group, turn]).astype(jnp.int32), cand_prompt, prompt_len, qkv, prompts
    )
    attended, block = lax.optimization_barrier((attended, block))
    block, weights[1], weights[3] = lax.optimization_barrier((block, weights[1], weights[3]))
    own = lax.all_to_all(
        attended.reshape(nz, -1, attended.shape[-1]), "z", 0, 0, tiled=True
    )
    own, last = lax.optimization_barrier((own, from_sides(block[None])))
    other = lax.ppermute(own, "core", swap)
    spots = jnp.stack([yh, lax.axis_index("z"), color]).astype(jnp.int32)
    local = lax.dynamic_slice(out_weight, (0, core * half_cols), (rows_here, half_cols))
    send, keep = project(spots, own, other, local, weights + last)
    summed = lax.ppermute(send, "yh", swap).astype(jnp.float32) + keep
    mine, theirs = summed[:per_device], summed[per_device:]
    back = lax.ppermute(theirs.astype(jnp.bfloat16), "core", swap).astype(jnp.float32)
    first = core == 0
    projected = jnp.concatenate(
        [jnp.where(first, mine, back), jnp.where(first, back, mine)], axis=1
    )
    spread = lax.rsqrt(jnp.mean(projected * projected, axis=-1, keepdims=True) + NORM_EPS)
    normed = projected * spread * post_gain
    return (residual.astype(jnp.float32) + normed[None]).astype(jnp.bfloat16)


def solution(mesh):
    fine = Mesh(mesh.devices.reshape(4, 2, 2, 8, 2), GROUP + SEQ)
    return jax.shard_map(
        body,
        mesh=fine,
        in_specs=(
            P(GROUP, SEQ, None),
            P(GROUP, SEQ, None, None),
            P(None, GROUP, SEQ, None),
            P(),
            P(),
            P(SEQ, None),
            P(),
        ),
        out_specs=P(GROUP, SEQ, None),
        check_vma=False,
    )
```

```python
import functools
import math

import jax
import jax.numpy as jnp
from jax import lax
from jax.experimental import pallas as pl
from jax.experimental.pallas import tpu as pltpu
from jax.sharding import Mesh, PartitionSpec as P

QUERY_SCALE = 144.0 ** (-0.5)
EXP2_SCALE = QUERY_SCALE / math.log(2.0)
NORM_EPS = 1e-06
NEG_FILL = -1e30
GROUP = ("x", "yl", "core")
SEQ = ("z", "yh")
MIB = 1 << 20
BLOCK_LOTS = ((1, -1, 2, -2, 3, -3), (4,))


def prepare_kernel(order_ref, kv_ref, weight_ref, picked_ref, piece_ref, sems):
    count = picked_ref.shape[0]
    rows, cols = piece_ref.shape
    color = (lax.axis_index("x") + 2 * lax.axis_index("yl")) % 4
    top = pl.multiple_of(color * rows, rows)
    left = pl.multiple_of(lax.axis_index("core") * cols, cols)
    copies = [
        pltpu.make_async_copy(
            weight_ref.at[pl.ds(top, rows), pl.ds(left, cols)], piece_ref, sems.at[count]
        )
    ]
    for i in range(count):
        copies.append(
            pltpu.make_async_copy(kv_ref.at[order_ref[i]], picked_ref.at[i], sems.at[i])
        )
    for copy in copies:
        copy.start()
    for copy in copies:
        copy.wait()


def prepare(order, kv, weight, rows, cols):
    smem = pl.BlockSpec(memory_space=pltpu.SMEM)
    vmem = pl.BlockSpec(memory_space=pltpu.VMEM)
    whole = pl.BlockSpec(memory_space=pltpu.HBM)
    return pl.pallas_call(
        prepare_kernel,
        out_shape=(
            jax.ShapeDtypeStruct(kv.shape, kv.dtype),
            jax.ShapeDtypeStruct((rows, cols), weight.dtype),
        ),
        in_specs=[smem, whole, whole],
        out_specs=(vmem, vmem),
        scratch_shapes=[pltpu.SemaphoreType.DMA((kv.shape[0] + 1,))],
        name="prepare",
    )(order, kv, weight)


def attend_kernel(spot_ref, order_ref, length_ref, qkv_ref, kv_ref, out_ref, own_v, prompt_v, *, block, chunk):
    tokens = qkv_ref.shape[0]
    places = kv_ref.shape[0]
    hd = 128
    dims = (((1,), (1,)), ((), ()))
    own_v[:, :hd] = qkv_ref[:, 3 * hd :]
    own_v[:, hd:] = jnp.ones((tokens, hd), jnp.bfloat16)
    prompt_v[:, :hd] = kv_ref[:, hd:]
    prompt_v[:, hd:] = jnp.ones((places, hd), jnp.bfloat16)
    limit = length_ref[order_ref[spot_ref[0]]]
    prompt_bias = jnp.where(
        lax.broadcasted_iota(jnp.int32, (1, places), 1) < limit, 0.0, NEG_FILL
    ).astype(jnp.float32)
    rows = lax.broadcasted_iota(jnp.int32, (block, block), 0)
    cols = lax.broadcasted_iota(jnp.int32, (block, block), 1)
    tri = jnp.where(cols <= rows, 0.0, NEG_FILL).astype(jnp.float32)
    tri = jnp.concatenate([tri, tri], axis=0)

    def scores(b):
        at = slice(b * block, (b + 1) * block)
        q = jnp.concatenate([qkv_ref[at, :hd], qkv_ref[at, hd : 2 * hd]], axis=0)
        score = functools.partial(
            lax.dot_general, q, dimension_numbers=dims, preferred_element_type=jnp.float32
        )
        pieces, values = [], []
        for c in range(0, places, chunk):
            part = slice(c, c + chunk)
            pieces.append(score(kv_ref[part, :hd]) + prompt_bias[:, part])
            values.append(prompt_v[part, :])
        if b > 0:
            pieces.append(score(qkv_ref[: b * block, 2 * hd : 3 * hd]))
            values.append(own_v[: b * block, :])
        pieces.append(score(qkv_ref[at, 2 * hd : 3 * hd]) + tri)
        values.append(own_v[at, :])
        return pieces, values

    def finish(b, pieces, values):
        at = slice(b * block, (b + 1) * block)
        top = functools.reduce(
            jnp.maximum, [jnp.max(s, axis=-1, keepdims=True) for s in pieces]
        )
        total = None
        for s, v in zip(pieces, values):
            w = jnp.exp2((s - top) * EXP2_SCALE).astype(jnp.bfloat16)
            part = jnp.dot(w, v, preferred_element_type=jnp.float32)
            total = part if total is None else total + part
        done = total[:, :hd] / total[:, hd:]
        done = jnp.concatenate([done[:block], done[block:]], axis=1)
        out_ref[at, :] = pltpu.roll(done, spot_ref[1], 1).astype(jnp.bfloat16)

    count = tokens // block
    coming = scores(0)
    for b in range(count):
        current = coming
        if b + 1 < count:
            coming = scores(b + 1)
        finish(b, *current)


def attend(spots, order, lengths, qkv, kv, block=256, chunk=512):
    tokens, places = qkv.shape[0], kv.shape[0]
    vmem = pl.BlockSpec(memory_space=pltpu.VMEM)
    return pl.pallas_call(
        functools.partial(attend_kernel, block=block, chunk=chunk),
        out_shape=jax.ShapeDtypeStruct((tokens, 256), jnp.bfloat16),
        in_specs=[pl.BlockSpec(memory_space=pltpu.SMEM)] * 3 + [vmem, vmem],
        out_specs=vmem,
        scratch_shapes=[
            pltpu.VMEM((tokens, 256), jnp.bfloat16),
            pltpu.VMEM((places, 256), jnp.bfloat16),
        ],
        compiler_params=pltpu.CompilerParams(vmem_limit_bytes=32 * MIB),
        cost_estimate=pl.CostEstimate(
            flops=10**6, bytes_accessed=MIB // 16, transcendentals=0
        ),
        name="attend",
    )(spots, order, lengths, qkv, kv)


def project_kernel(spot_ref, own_ref, other_ref, local, *refs):
    weights, (send_ref, send_other_ref, keep_ref, total) = refs[:-4], refs[-4:]
    blocks = own_ref.shape[0]
    rows, cols = local.shape
    quarter = rows // 4
    half = own_ref.shape[1] // 2
    here = pl.multiple_of(spot_ref[0] * half, half)
    there = pl.multiple_of((1 - spot_ref[0]) * half, half)
    width = 256
    places = [(d, lot, k) for lot, distances in enumerate(BLOCK_LOTS) for k, d in enumerate(distances)]
    places.append((0, None, None))
    for r, (distance, lot, k) in enumerate(places):
        n = lax.rem(spot_ref[1] + distance + blocks, blocks)
        tokens = jnp.concatenate(
            [ref[n, pl.ds(at, half), :] for at in (there, here) for ref in (own_ref, other_ref)],
            axis=0,
        )
        for j in range(cols // width):
            at = slice(j * width, (j + 1) * width)
            if lot is None:
                quarters = []
                for i in range(4):
                    top = pl.multiple_of(lax.rem(spot_ref[2] + i, 4) * quarter, quarter)
                    quarters.append(local[pl.ds(top, quarter), at])
            else:
                quarters = [weights[4 * lot + i][k, :, at] for i in range(4)]
            part = jnp.dot(
                tokens, jnp.concatenate(quarters, axis=0), preferred_element_type=jnp.float32
            )
            if r > 0:
                part = part + total[:, at]
            if r < blocks - 1:
                total[:, at] = part
            else:
                send_ref[:, at] = part[:half].astype(jnp.bfloat16)
                send_other_ref[:, at] = part[half : 2 * half].astype(jnp.bfloat16)
                keep_ref[:, at] = part[2 * half :]


def project(spots, own, other, local, weights):
    vmem = pl.BlockSpec(memory_space=pltpu.VMEM)
    quarter, cols = weights[0].shape[1:]
    blocks, tokens = own.shape[:2]
    return pl.pallas_call(
        project_kernel,
        out_shape=(
            jax.ShapeDtypeStruct((tokens // 2, cols), jnp.bfloat16),
            jax.ShapeDtypeStruct((tokens // 2, cols), jnp.bfloat16),
            jax.ShapeDtypeStruct((tokens, cols), jnp.float32),
        ),
        in_specs=[pl.BlockSpec(memory_space=pltpu.SMEM)] + [vmem] * (3 + len(weights)),
        out_specs=(vmem, vmem, vmem),
        scratch_shapes=[
            pltpu.VMEM((2 * tokens, cols), jnp.float32),
        ],
        compiler_params=pltpu.CompilerParams(vmem_limit_bytes=32 * MIB),
        cost_estimate=pl.CostEstimate(
            flops=2 * 2 * tokens * blocks * 4 * quarter * cols,
            bytes_accessed=12 * MIB,
            transcendentals=0,
        ),
        name="project",
    )(spots, own, other, local, *weights)


def body(residual, cand_qkv, prompt_kv, prompt_len, cand_prompt, out_weight, post_gain):
    x, yl, core = (lax.axis_index(n) for n in GROUP)
    yh = lax.axis_index("yh")
    nx, nz = lax.axis_size("x"), lax.axis_size("z")
    group = lax.axis_index(GROUP)
    per_device, heads, width = cand_qkv.shape[1:]
    features = residual.shape[-1]
    half_cols = features // 2
    rows_here = out_weight.shape[0]
    quarter = rows_here // 4

    color = (x + 2 * yl) % 4
    picked, piece = prepare(
        cand_prompt,
        prompt_kv.reshape(prompt_kv.shape[0], prompt_kv.shape[1], -1),
        out_weight,
        quarter,
        half_cols,
    )
    def from_z(block, distance):
        return lax.ppermute(block, "z", [((i + distance) % nz, i) for i in range(nz)])

    def from_sides(lot):
        return [
            lot,
            lax.ppermute(lot, "x", [(i, (i - 1) % nx) for i in range(nx)]),
            lax.ppermute(lot, "yl", swap),
            lax.ppermute(lot, "x", [(i, (i + 1) % nx) for i in range(nx)]),
        ]

    swap = [(0, 1), (1, 0)]
    blocks = {0: piece, **{d: from_z(piece, d) for d in (1, -1, 2, -2)}}
    blocks.update({3: from_z(blocks[2], 1), -3: from_z(blocks[-2], -1)})
    near = jnp.stack([blocks[d] for d in BLOCK_LOTS[0]])
    prompts = lax.all_to_all(picked, GROUP, 0, 0, tiled=True)
    prompts = prompts.reshape(-1, prompts.shape[-1])
    by_head = cand_qkv[0].transpose(1, 0, 2)
    by_head, prompts, near = lax.optimization_barrier((by_head, prompts, near))
    qkv = lax.all_to_all(by_head, SEQ, 0, 0, tiled=True).reshape(-1, width)
    weights = from_sides(near)
    qkv, block = lax.optimization_barrier((qkv, blocks[3]))
    block = from_z(block, 1)

    turn = (4 - color) % 4 * quarter
    attended = attend(
        jnp.stack([group, turn]).astype(jnp.int32), cand_prompt, prompt_len, qkv, prompts
    )
    attended, block = lax.optimization_barrier((attended, block))
    block, weights[1], weights[3] = lax.optimization_barrier((block, weights[1], weights[3]))
    own = lax.all_to_all(
        attended.reshape(nz, -1, attended.shape[-1]), "z", 0, 0, tiled=True
    )
    own, last = lax.optimization_barrier((own, from_sides(block[None])))
    other = lax.ppermute(own, "core", swap)
    spots = jnp.stack([yh, lax.axis_index("z"), color]).astype(jnp.int32)
    local = lax.dynamic_slice(out_weight, (0, core * half_cols), (rows_here, half_cols))
    send, send_other, keep = project(spots, own, other, local, weights + last)
    theirs = lax.ppermute(send_other, "yh", swap)
    theirs = theirs.astype(jnp.float32) + keep[per_device:]
    back = lax.ppermute(theirs.astype(jnp.bfloat16), "core", swap).astype(jnp.float32)
    mine = lax.ppermute(send, "yh", swap).astype(jnp.float32) + keep[:per_device]
    first = core == 0
    projected = jnp.concatenate(
        [jnp.where(first, mine, back), jnp.where(first, back, mine)], axis=1
    )
    spread = lax.rsqrt(jnp.mean(projected * projected, axis=-1, keepdims=True) + NORM_EPS)
    normed = projected * spread * post_gain
    return (residual.astype(jnp.float32) + normed[None]).astype(jnp.bfloat16)


def solution(mesh):
    fine = Mesh(mesh.devices.reshape(4, 2, 2, 8, 2), GROUP + SEQ)
    return jax.shard_map(
        body,
        mesh=fine,
        in_specs=(
            P(GROUP, SEQ, None),
            P(GROUP, SEQ, None, None),
            P(None, GROUP, SEQ, None),
            P(),
            P(),
            P(SEQ, None),
            P(),
        ),
        out_specs=P(GROUP, SEQ, None),
        check_vma=False,
    )
```
